768 devices in a mesh: dp: 16 (over y, core), expert: 48 (over z, x).
Axes of the slice: x: 4, y: 8, z: 12, core: 2. Of those that a mesh axis runs over, the one named last changes fastest.
Arguments:
- tokens: bfloat16 [12288, 7168], P('expert', 'dp'), may hold values from -6 to 6
- cotangent: bfloat16 [12288, 7168], P('expert', 'dp'), may hold values from -1.796875 to 1.796875
- expert_ids: int32 [12288, 8], P('expert'), may hold values from 0 to 255, as said below
- route_probs: bfloat16 [12288, 8], P('expert'), may hold values from 0.099609375 to 1
- w_up: bfloat16 [48, 7168, 1024], P('expert', 'dp'), may hold values from -0.0625 to 0.0625
- w_down: bfloat16 [48, 1024, 7168], P('expert', None, 'dp'), may hold values from -0.1875 to 0.1875
Outputs:
- grad_tokens: bfloat16 [12288, 7168], P('expert', 'dp')
- grad_probs: bfloat16 [12288, 8], P('expert')
- grad_up: bfloat16 [48, 7168, 1024], P('expert', 'dp')
- grad_down: bfloat16 [48, 1024, 7168], P('expert', None, 'dp')
The draws below stay inside these ranges and needn't reach their ends.
Inputs may be any that keep to these rules, and one draw needn't show every extreme that they name: `expert_ids`: A token names each id at most once. Within one block of 256 tokens each id below 48 is named by at most 8 tokens; one such id is named by exactly 8 tokens in every block, and in most blocks another one too; loads of the ids below 48 are strongly uneven.
All inputs are finite; a program needn't handle non-finite values.
Results may differ from the reference program's by a relative error of at most 0.008.
Values may be sent and summed in bfloat16 or wider, within the bound.
A program may use at most 32 MiB of HBM per device.

```python
import jax
import jax.numpy as jnp
from jax import lax

D = 7168
FF = 1024
ROUTED = 256
TOP = 8
CAP = 8
TOK_DEV = 256
EXPERTS = 48
SLABS = 16
TOKENS = 12288


def draw_expert_ids(key, part):
    block_count = TOKENS // TOK_DEV
    hot_key, rest_key = jax.random.split(key)
    hot_global = jax.random.randint(hot_key, (), 0, EXPERTS)
    block_keys = jax.random.split(rest_key, block_count)

    def one_block(block_key):
        sub_keys = jax.random.split(block_key, 6)
        first = jax.random.randint(sub_keys[0], (EXPERTS,), 0, CAP + 1)
        second = jax.random.randint(sub_keys[1], (EXPERTS,), 0, CAP + 1)
        counts = first * second // CAP
        hot_local = jax.random.randint(sub_keys[2], (), 0, EXPERTS)
        expert_index = jnp.arange(EXPERTS, dtype=jnp.int32)
        counts = jnp.where((expert_index == hot_global) | (expert_index == hot_local), CAP, counts)
        starts = jnp.cumsum(counts) - counts
        positions = jnp.arange(TOP * TOK_DEV, dtype=jnp.int32)
        inside = (positions[:, None] >= starts[None, :]) & (positions[:, None] < (starts + counts)[None, :])
        owner_id = jnp.sum(jnp.where(inside, expert_index[None, :], 0), axis=1)
        is_live = jnp.any(inside, axis=1)
        offset_draw = jax.random.randint(sub_keys[3], (TOK_DEV,), 0, ROUTED - EXPERTS)
        layer_of = positions // TOK_DEV
        token_of = positions % TOK_DEV
        outside = EXPERTS + (offset_draw[token_of] + layer_of) % (ROUTED - EXPERTS)
        id_grid = jnp.where(is_live, owner_id, outside).reshape(TOP, TOK_DEV).T
        token_order = jax.random.permutation(sub_keys[4], TOK_DEV)
        id_grid = id_grid[token_order]
        scores = jax.random.randint(sub_keys[5], (TOK_DEV, TOP), 0, 1024) * TOP + jnp.arange(TOP, dtype=jnp.int32)[None, :]
        column_order = jnp.argsort(scores, axis=1)
        return jnp.take_along_axis(id_grid, column_order, axis=1)
    return jax.vmap(one_block)(block_keys).reshape(TOKENS, TOP).astype(jnp.int32)


def level_of(stream_key, dims, shards, smallest, largest):
    loudness, own = 1.0, jax.random.fold_in(stream_key, 6)
    for axis_at, parts in shards:
        heights = jnp.exp(jax.random.uniform(jax.random.fold_in(own, axis_at), (parts,), jnp.float32, smallest / len(shards), largest / len(shards)))
        loudness = loudness * jnp.repeat(heights, dims[axis_at] // parts).reshape([-1 if axis == axis_at else 1 for axis in range(len(dims))])
    return loudness


def centred(rng, dims, scale, limit, shards=(), kind=jnp.bfloat16):
    values = jax.random.normal(rng, dims, jnp.float32) * scale
    if len(shards) > 0:
        values = level_of(rng, dims, shards, -0.22, 0.18) * values
    return jnp.clip(values, min=-limit, max=limit).astype(kind)


def setup_inputs(seed: int = 0) -> dict:
    streams_of = jax.random.split(jax.random.key(seed), 7)
    return {
        "tokens": centred(streams_of[0], (TOKENS, D), 1.0, 6.0, ((0, 48), (1, 16))),
        "cotangent": centred(streams_of[1], (TOKENS, D), 0.3, 1.796875, ((0, 48), (1, 16))),
        "expert_ids": draw_expert_ids(jax.random.fold_in(streams_of[6], 71), 0),
        "route_probs": jnp.clip(0.099609375 + 0.9003906 * jax.random.uniform(streams_of[3], (TOKENS, TOP), jnp.float32) ** level_of(streams_of[3], (TOKENS, TOP), ((0, 48),), -0.2, 0.2), 0.099609375, 1.0).astype(jnp.bfloat16),
        "w_up": centred(streams_of[4], (EXPERTS, D, FF), D ** -0.5, 0.0625, ((0, 48), (1, 16))),
        "w_down": centred(streams_of[5], (EXPERTS, FF, D), FF ** -0.5, 0.1875, ((0, 48), (2, 16))),
    }


def sum_blocks(partials):
    return jnp.sum(partials, axis=0)


def reference(tokens, cotangent, expert_ids, route_probs, w_up, w_down):
    row_total = EXPERTS * CAP
    slab_width = D // SLABS
    numbers = jnp.arange(EXPERTS, dtype=jnp.int32)
    chosen = (expert_ids[:, :, None] == numbers[None, None, :]).astype(jnp.int32)
    per_token = jnp.sum(chosen, axis=1).reshape(EXPERTS, TOK_DEV, EXPERTS)
    before = (jnp.cumsum(per_token, axis=1) - per_token).reshape(TOKENS, EXPERTS)
    order_rank = jnp.sum(chosen * before[:, None, :], axis=2)
    block_of = (jnp.arange(TOKENS, dtype=jnp.int32) // TOK_DEV)[:, None]
    target = jnp.where(expert_ids < EXPERTS, expert_ids * row_total + block_of * CAP + order_rank, EXPERTS * row_total)
    slot_ids = jnp.arange(TOKENS * TOP, dtype=jnp.int32)
    table = jnp.full((EXPERTS * row_total,), TOKENS * TOP, jnp.int32)
    table = table.at[target.reshape(-1).astype(jnp.int32)].set(slot_ids, mode="drop").reshape(EXPERTS, row_total)
    token_pad = jnp.concatenate([tokens, jnp.zeros((1, D), tokens.dtype)], axis=0)
    cot_pad = jnp.concatenate([cotangent, jnp.zeros((1, D), cotangent.dtype)], axis=0)
    prob_pad = jnp.concatenate([route_probs.reshape(-1), jnp.zeros((1,), route_probs.dtype)], axis=0)

    def expert_step(carry, inputs):
        grad_acc, prob_acc = carry
        slot_rows, up_weight, down_weight = inputs
        token_of = jnp.minimum(slot_rows // TOP, TOKENS).astype(jnp.int32)
        rows_x = token_pad[token_of]
        rows_dy = cot_pad[token_of]
        gate_rows = prob_pad[slot_rows].astype(jnp.float32)
        hidden = sum_blocks(jnp.einsum("rjd,jdf->jrf", rows_x.reshape(row_total, SLABS, slab_width).astype(jnp.float32), up_weight.reshape(SLABS, slab_width, FF).astype(jnp.float32)))
        query = sum_blocks(jnp.einsum("rjd,fjd->jrf", rows_dy.reshape(row_total, SLABS, slab_width).astype(jnp.float32), down_weight.reshape(FF, SLABS, slab_width).astype(jnp.float32)))
        sigma_h = jax.nn.sigmoid(hidden)
        act_rows = (hidden * sigma_h).astype(jnp.bfloat16)
        score_rows = jnp.sum(act_rows.astype(jnp.float32) * query, axis=1).astype(jnp.bfloat16)
        hidden_grad = (gate_rows[:, None] * query * sigma_h * (1.0 + hidden * (1.0 - sigma_h))).astype(jnp.bfloat16)
        scaled = (gate_rows[:, None] * rows_dy.astype(jnp.float32)).astype(jnp.bfloat16)
        row_grad = jnp.dot(hidden_grad, up_weight.T, preferred_element_type=jnp.float32).astype(jnp.bfloat16)
        grad_acc = grad_acc.at[token_of].add(row_grad.astype(jnp.float32))
        prob_acc = prob_acc.at[slot_rows].add(score_rows.astype(jnp.float32))
        grad_upper = jnp.dot(rows_x.T, hidden_grad, preferred_element_type=jnp.float32).astype(jnp.bfloat16)
        grad_lower = jnp.dot(act_rows.T, scaled, preferred_element_type=jnp.float32).astype(jnp.bfloat16)
        return (grad_acc, prob_acc), (grad_upper, grad_lower)

    start = (jnp.zeros((TOKENS + 1, D), jnp.float32), jnp.zeros((TOKENS * TOP + 1,), jnp.float32))
    (grad_acc, prob_acc), (grad_up, grad_down) = lax.scan(expert_step, start, (table, w_up, w_down))
    grad_tokens = grad_acc[:TOKENS].astype(jnp.bfloat16)
    grad_probs = prob_acc[:TOKENS * TOP].reshape(TOKENS, TOP).astype(jnp.bfloat16)
    return (grad_tokens, grad_probs, grad_up, grad_down)
```

```python
import functools

import jax
import jax.numpy as jnp
from jax import lax
from jax.experimental import pallas as pl
from jax.experimental.pallas import tpu as pltpu
from jax.sharding import PartitionSpec as P

CAP = 8
MSG = 16
HALF = 256
STEP = 256
MESH = pl.DeviceIdType.MESH
BF16, F32 = jnp.bfloat16, jnp.float32


def dot(left, right, left_dim=1, right_dim=0):
    return lax.dot_general(
        left, right, (((left_dim,), (right_dim,)), ((), ())), preferred_element_type=F32
    )


def iota(shape, dim):
    return lax.broadcasted_iota(jnp.int32, shape, dim)


def kernel(
    experts,
    chips,
    tok_ref,
    cot_ref,
    ids_ref,
    prob_ref,
    up_hbm,
    down_hbm,
    gtok_ref,
    gprob_ref,
    gup_ref,
    gdown_ref,
    send_x,
    send_dy,
    got_x,
    got_dy,
    up,
    down,
    rows_x,
    rows_dy,
    part_h,
    part_q,
    own_h,
    own_q,
    sum_h,
    sum_q,
    hgrad,
    actg,
    score,
    ret,
    back,
    held,
    load_sem,
    send_sem,
    recv_sem,
):
    d = lax.axis_index("dp")
    g = lax.axis_index("expert")
    y, c = d // 2, lax.rem(d, 2)
    sib = 2 * y + 1 - c
    parity = lax.rem(g, 2)
    slot = lax.rem(c + parity, 2)
    block, feat = tok_ref.shape
    top = ids_ref.shape[1]
    ff = up_hbm.shape[1]
    rows = experts * CAP
    half = rows // 2
    blocks = experts // 2
    high = feat - HALF

    load_up = pltpu.make_async_copy(up_hbm, up.at[0, pl.ds(0, feat)], load_sem.at[0])
    load_down = pltpu.make_async_copy(down_hbm, down.at[0], load_sem.at[1])
    load_up.start()
    load_down.start()

    barrier = pltpu.get_barrier_semaphore()

    def greet(i, carry):
        e = lax.rem(g + i, experts)
        pl.semaphore_signal(barrier, inc=1, device_id=(d, e), device_id_type=MESH)
        pl.semaphore_signal(barrier, inc=1, device_id=(sib, e), device_id_type=MESH)
        return carry

    lax.fori_loop(1, experts, greet, 0)
    pl.semaphore_signal(barrier, inc=1, device_id=(sib, g), device_id_type=MESH)
    for i in range(1, chips):
        peer = lax.rem(y + i, chips) * 2 + c
        pl.semaphore_signal(barrier, inc=1, device_id=(peer, g), device_id_type=MESH)

    ids = ids_ref[...]
    probs = prob_ref[...].astype(F32)
    lane = iota((block, 128), 1)
    lane_hi = iota((block, HALF), 1)
    named = jnp.zeros((block, 128), F32)
    gates = jnp.zeros((block, HALF), F32)
    for k in range(top):
        column = ids[:, k : k + 1]
        named = named + jnp.where((column == lane) & (lane < experts), 1.0, 0.0)
        gates = gates + jnp.where(column == lane_hi - high, probs[:, k : k + 1], 0.0)
    named = named.astype(BF16)
    earlier = jnp.where(iota((block, block), 1) < iota((block, block), 0), 1.0, 0.0).astype(BF16)
    before = dot(earlier, named).astype(BF16)
    spread_t = jnp.where(iota((rows, 128), 0) // CAP == iota((rows, 128), 1), 1.0, 0.0).astype(BF16)
    named_t = dot(spread_t, named, 1, 1)
    before_t = dot(spread_t, before, 1, 1)
    place_t = jnp.where(
        (named_t > 0.5) & (before_t == lax.rem(iota((rows, block), 0), CAP).astype(F32)), 1.0, 0.0
    ).astype(BF16)
    spread = jnp.where(iota((128, rows), 1) // CAP == iota((128, rows), 0), 1.0, 0.0).astype(BF16)
    held[...] = jnp.where(
        (dot(named, spread) > 0.5)
        & (dot(before, spread) == lax.rem(iota((block, rows), 1), CAP).astype(F32)),
        1.0,
        0.0,
    ).astype(BF16)

    widen = jnp.where(iota((high, HALF), 0) == iota((high, HALF), 1), 1.0, 0.0).astype(BF16)

    def pack(low, hi, count):
        return jnp.concatenate(
            [low.reshape(count, CAP, HALF), hi.reshape(count, CAP, HALF)], axis=1
        ).astype(BF16)

    def unpack(message, count):
        wide = message.astype(F32)
        return (
            wide[:, :CAP].reshape(count * CAP, HALF),
            wide[:, CAP:].reshape(count * CAP, HALF),
        )

    tok_hi = (dot(tok_ref[:, HALF:], widen) + gates).astype(BF16)
    send_x[...] = pack(dot(place_t, tok_ref[:, :HALF]), dot(place_t, tok_hi), experts)
    cot_hi = dot(cot_ref[:, HALF:], widen).astype(BF16)
    send_dy[...] = pack(dot(place_t, cot_ref[:, :HALF]), dot(place_t, cot_hi), experts)
    for s in range(2):
        up[s, feat:, :] = jnp.zeros((2 * HALF - feat, ff), BF16)

    pl.semaphore_wait(barrier, 2 * experts - 1 + chips - 1)

    def dispatch(source, target, n):
        def remote(e, core):
            return pltpu.make_async_remote_copy(
                src_ref=source.at[e],
                dst_ref=target.at[slot, g // 2],
                send_sem=send_sem.at[n],
                recv_sem=recv_sem.at[n],
                device_id=(core, e),
                device_id_type=MESH,
            )

        def body(i, carry):
            remote(lax.rem(g + i, experts), 2 * y + parity).start()
            return carry

        lax.fori_loop(1, experts, body, 0)

        @pl.when(c == parity)
        def _():
            pltpu.make_async_copy(source.at[g], target.at[0, g // 2], recv_sem.at[n]).start()

        @pl.when(c != parity)
        def _():
            remote(g, sib).start()

    def to_sibling(source, target, n):
        copy = pltpu.make_async_remote_copy(
            src_ref=source,
            dst_ref=target,
            send_sem=send_sem.at[n],
            recv_sem=recv_sem.at[n],
            device_id=(sib, g),
            device_id_type=MESH,
        )
        copy.start()
        return copy

    def arrived(buffer, n):
        pltpu.make_async_copy(buffer, buffer, recv_sem.at[n]).wait()

    def sent(buffer, n):
        pltpu.make_async_copy(buffer, buffer, send_sem.at[n]).wait()

    dispatch(send_x, got_x, 0)
    load_up.wait()
    load_down.wait()
    up_copy = to_sibling(up.at[0, pl.ds(0, feat)], up.at[1, pl.ds(0, feat)], 2)
    down_copy = to_sibling(down.at[0], down.at[1], 3)
    dispatch(send_dy, got_dy, 1)

    turns = [chips // 2]
    for i in range(1, (chips + 1) // 2):
        turns += [i, chips - i]

    def to_peers(source_of, target, n):
        for i in turns:
            peer = lax.rem(y + i, chips)
            pltpu.make_async_remote_copy(
                src_ref=source_of(peer),
                dst_ref=target,
                send_sem=send_sem.at[n],
                recv_sem=recv_sem.at[n],
                device_id=(peer * 2 + c, g),
                device_id_type=MESH,
            ).start()

    unit = ff // chips

    arrived(got_x, 0)
    low, hi = unpack(got_x[0], blocks)
    gate = jnp.sum(jnp.where(iota((half, HALF), 1) == g + high, hi, 0.0), axis=1, keepdims=True)
    rows_x[0] = jnp.concatenate([low, hi], axis=1).astype(BF16)
    low, hi = unpack(got_x[1], blocks)
    rows_x[2] = jnp.concatenate([low, hi], axis=1).astype(BF16)
    up_copy.wait()
    for n in range(ff // STEP):
        cols = pl.ds(n * STEP, STEP)
        product = dot(rows_x[0], up[0, :, cols]) + dot(rows_x[2], up[1, :, cols])
        for m in range(STEP // unit):
            piece = product[:, m * unit : (m + 1) * unit]
            own_h[n * (STEP // unit) + m] = piece
            part_h[n * (STEP // unit) + m] = piece.astype(BF16)
    to_peers(lambda peer: part_h.at[peer], sum_h.at[y], 4)
    x_copy = to_sibling(rows_x.at[2], rows_x.at[1], 5)

    arrived(got_dy, 1)
    for s in range(2):
        low, hi = unpack(got_dy[s], blocks)
        rows_dy[2 * s] = jnp.concatenate([low, hi], axis=1).astype(BF16)
    down_copy.wait()
    for n in range(ff // STEP):
        part = pl.ds(n * STEP, STEP)
        product = dot(rows_dy[0, :, :feat], down[0, part, :], 1, 1) + dot(
            rows_dy[2, :, :feat], down[1, part, :], 1, 1
        )
        for m in range(STEP // unit):
            piece = product[:, m * unit : (m + 1) * unit]
            own_q[n * (STEP // unit) + m] = piece
            part_q[n * (STEP // unit) + m] = piece.astype(BF16)
    to_peers(lambda peer: part_q.at[peer], sum_q.at[y], 6)
    dy_copy = to_sibling(rows_dy.at[2], rows_dy.at[1], 7)

    arrived(sum_h.at[pl.ds(0, chips - 1)], 4)
    hidden = own_h[y]
    for i in range(1, chips):
        hidden = hidden + sum_h[lax.rem(y + i, chips)].astype(F32)
    sigma = jax.nn.sigmoid(hidden)
    act = (hidden * sigma).astype(BF16).astype(F32)
    slope = gate * (sigma * (1.0 + hidden * (1.0 - sigma)))
    arrived(sum_q.at[pl.ds(0, chips - 1)], 6)
    query = own_q[y]
    for i in range(1, chips):
        query = query + sum_q[lax.rem(y + i, chips)].astype(F32)
    hgrad[0, y] = (slope * query).astype(BF16)
    to_peers(lambda peer: hgrad.at[0, y], hgrad.at[0, y], 8)
    score[y] = lax.dot_general(
        jnp.ones((8, unit), F32),
        act * query,
        (((1,), (1,)), ((), ())),
        precision=lax.Precision.HIGHEST,
        preferred_element_type=F32,
    )
    to_peers(lambda peer: score.at[y], score.at[y], 9)
    actg[0, y] = (gate * act).astype(BF16)
    to_peers(lambda peer: actg.at[0, y], actg.at[0, y], 10)

    arrived(hgrad.at[0, pl.ds(0, chips - 1)], 8)
    hgrad_copy = to_sibling(hgrad.at[0], hgrad.at[1], 11)
    arrived(score.at[pl.ds(0, chips - 1)], 9)
    total = score[0]
    for i in range(1, chips):
        total = total + score[i]
    mark = jnp.where(
        (iota((8, HALF), 0) == 0) & (iota((8, HALF), 1) == g + high), 1.0, 0.0
    ).astype(BF16)
    score_lane = dot(total.astype(BF16), mark, 0, 0)
    grad_rows = jnp.concatenate([hgrad[0, i] for i in range(chips)], axis=1)
    for s in range(2):
        low = dot(grad_rows, up[s, :HALF, :], 1, 1)
        hi = dot(grad_rows, up[s, HALF:, :], 1, 1) + score_lane
        ret[s] = pack(low, hi, blocks)

    def remote_back(s, j, core, b):
        return pltpu.make_async_remote_copy(
            src_ref=ret.at[s, j],
            dst_ref=back.at[g],
            send_sem=send_sem.at[12],
            recv_sem=recv_sem.at[12],
            device_id=(core, b),
            device_id_type=MESH,
        )

    def body(i, carry):
        j = lax.rem(g // 2 + i, blocks)
        b = 2 * j + c
        remote_back(0, j, d, b).start()
        remote_back(1, j, sib, b).start()
        return carry

    lax.fori_loop(1, blocks, body, 0)
    first = 2 * (g // 2) + c
    remote_back(1, g // 2, sib, first).start()

    @pl.when(c == parity)
    def _():
        pltpu.make_async_copy(ret.at[0, g // 2], back.at[g], recv_sem.at[12]).start()

    @pl.when(c != parity)
    def _():
        remote_back(0, g // 2, d, first).start()

    x_copy.wait()
    hgrad_copy.wait()
    own_x = jnp.concatenate([rows_x[0], rows_x[1]], axis=0)
    for n in range(ff // STEP):
        units = range(n * (STEP // unit), (n + 1) * (STEP // unit))
        right = jnp.concatenate(
            [jnp.concatenate([hgrad[0, i], hgrad[1, i]], axis=0) for i in units], axis=1
        )
        gup_ref[:, pl.ds(n * STEP, STEP)] = dot(own_x, right, 0, 0)[:feat].astype(BF16)
    arrived(actg.at[0, pl.ds(0, chips - 1)], 10)
    actg_copy = to_sibling(actg.at[0], actg.at[1], 13)
    dy_copy.wait()
    own_dy = jnp.concatenate([rows_dy[0], rows_dy[1]], axis=0)
    actg_copy.wait()
    for n in range(ff // STEP):
        units = range(n * (STEP // unit), (n + 1) * (STEP // unit))
        left = jnp.concatenate(
            [jnp.concatenate([actg[0, i], actg[1, i]], axis=0) for i in units], axis=1
        )
        gdown_ref[pl.ds(n * STEP, STEP), :] = dot(left, own_dy, 0, 0)[:, :feat].astype(BF16)

    arrived(back, 12)
    low, hi = unpack(back[...], experts)
    gtok_ref[:, :HALF] = dot(held[...], low.astype(BF16)).astype(BF16)
    top_lanes = dot(held[...], hi.astype(BF16))
    gtok_ref[:, HALF:] = top_lanes[:, :high].astype(BF16)
    found = jnp.zeros((block, top), F32)
    for k in range(top):
        value = jnp.sum(
            jnp.where((ids[:, k : k + 1] == lane_hi - high) & (lane_hi >= high), top_lanes, 0.0),
            axis=1,
            keepdims=True,
        )
        found = found + jnp.where(iota((block, top), 1) == k, value, 0.0)
    gprob_ref[...] = found.astype(BF16)

    for n, buffer in ((0, send_x), (1, send_dy), (12, back)):

        @pl.when(c == parity)
        def _(n=n, buffer=buffer):
            sent(buffer.at[pl.ds(0, experts - 1)], n)

        @pl.when(c != parity)
        def _(n=n, buffer=buffer):
            sent(buffer, n)

    for n, buffer in ((4, sum_h), (6, sum_q), (8, hgrad.at[0]), (9, score), (10, actg.at[0])):
        sent(buffer.at[pl.ds(0, chips - 1)], n)


def on_device(tokens, cotangent, expert_ids, route_probs, w_up, w_down):
    experts = lax.axis_size("expert")
    chips = lax.axis_size("dp") // 2
    block, feat = tokens.shape
    top = expert_ids.shape[1]
    ff = w_up.shape[2]
    half = experts * CAP // 2
    blocks = experts // 2
    unit = ff // chips
    wide = 2 * HALF
    vmem = pl.BlockSpec(memory_space=pltpu.VMEM)
    anywhere = pl.BlockSpec(memory_space=pl.ANY)
    grad_tokens, grad_probs, grad_up, grad_down = pl.pallas_call(
        functools.partial(kernel, experts, chips),
        out_shape=(
            jax.ShapeDtypeStruct((block, feat), BF16),
            jax.ShapeDtypeStruct((block, top), BF16),
            jax.ShapeDtypeStruct((feat, ff), BF16),
            jax.ShapeDtypeStruct((ff, feat), BF16),
        ),
        in_specs=[vmem] * 4 + [anywhere] * 2,
        out_specs=[vmem] * 4,
        scratch_shapes=[
            pltpu.VMEM((experts, MSG, HALF), BF16),
            pltpu.VMEM((experts, MSG, HALF), BF16),
            pltpu.VMEM((2, blocks, MSG, HALF), BF16),
            pltpu.VMEM((2, blocks, MSG, HALF), BF16),
            pltpu.VMEM((2, wide, ff), BF16),
            pltpu.VMEM((2, ff, feat), BF16),
            pltpu.VMEM((3, half, wide), BF16),
            pltpu.VMEM((3, half, wide), BF16),
            pltpu.VMEM((chips, half, unit), BF16),
            pltpu.VMEM((chips, half, unit), BF16),
            pltpu.VMEM((chips, half, unit), F32),
            pltpu.VMEM((chips, half, unit), F32),
            pltpu.VMEM((chips, half, unit), BF16),
            pltpu.VMEM((chips, half, unit), BF16),
            pltpu.VMEM((2, chips, half, unit), BF16),
            pltpu.VMEM((2, chips, half, unit), BF16),
            pltpu.VMEM((chips, 8, half), F32),
            pltpu.VMEM((2, blocks, MSG, HALF), BF16),
            pltpu.VMEM((experts, MSG, HALF), BF16),
            pltpu.VMEM((block, experts * CAP), BF16),
            pltpu.SemaphoreType.DMA((2,)),
            pltpu.SemaphoreType.DMA((14,)),
            pltpu.SemaphoreType.DMA((14,)),
        ],
        compiler_params=pltpu.CompilerParams(
            collective_id=0, has_side_effects=True, vmem_limit_bytes=56 * 2**20
        ),
        name="expert_backward",
    )(tokens, cotangent, expert_ids, route_probs, w_up[0], w_down[0])
    return (grad_tokens, grad_probs, grad_up[None], grad_down[None])


def solution(mesh):
    in_specs = (
        P("expert", "dp"),
        P("expert", "dp"),
        P("expert", None),
        P("expert", None),
        P("expert", "dp", None),
        P("expert", None, "dp"),
    )
    out_specs = (
        P("expert", "dp"),
        P("expert", None),
        P("expert", "dp", None),
        P("expert", None, "dp"),
    )
    return jax.shard_map(
        on_device, mesh=mesh, in_specs=in_specs, out_specs=out_specs, check_vma=False
    )
```

```python
import functools

import jax
import jax.numpy as jnp
from jax import lax
from jax.experimental import pallas as pl
from jax.experimental.pallas import tpu as pltpu
from jax.sharding import PartitionSpec as P

CAP = 8
MSG = 16
HALF = 256
STEP = 256
ROW = 4
MESH = pl.DeviceIdType.MESH
BF16, F32 = jnp.bfloat16, jnp.float32


def dot(left, right, left_dim=1, right_dim=0):
    return lax.dot_general(
        left, right, (((left_dim,), (right_dim,)), ((), ())), preferred_element_type=F32
    )


def iota(shape, dim):
    return lax.broadcasted_iota(jnp.int32, shape, dim)


def kernel(
    experts,
    chips,
    tok_hbm,
    cot_hbm,
    ids_hbm,
    prob_hbm,
    up_hbm,
    down_hbm,
    gtok_ref,
    gprob_ref,
    gup_ref,
    gdown_ref,
    tok_ref,
    cot_ref,
    ids_ref,
    prob_ref,
    send_x,
    send_dy,
    got_x,
    got_dy,
    up,
    down,
    rows_x,
    rows_dy,
    part_h,
    part_q,
    own_h,
    own_q,
    sum_h,
    sum_q,
    hgrad,
    actg,
    score,
    ret,
    back,
    held,
    load_sem,
    send_sem,
    recv_sem,
):
    d = lax.axis_index("dp")
    g = lax.axis_index("expert")
    y, c = d // 2, lax.rem(d, 2)
    sib = 2 * y + 1 - c
    parity = lax.rem(g, 2)
    slot = lax.rem(c + parity, 2)
    feat, block = tok_hbm.shape
    top = ids_hbm.shape[0]
    ff = up_hbm.shape[1]
    rows = experts * CAP
    half = rows // 2
    blocks = experts // 2
    high = feat - HALF
    rings = experts // ROW
    z, x = g // ROW, lax.rem(g, ROW)
    part = half // 2
    place_of_mine = (x // 2) * rings + z

    def far_first(i):
        j = rings - 1 - i
        near = (j + 1) // 2
        return lax.rem(z + jnp.where(lax.rem(j, 2) == 1, near, rings - near), rings)

    loads = [
        pltpu.make_async_copy(source, target, load_sem.at[n])
        for n, (source, target) in enumerate(
            (
                (ids_hbm, ids_ref),
                (prob_hbm, prob_ref),
                (tok_hbm, tok_ref),
                (cot_hbm, cot_ref),
                (up_hbm, up.at[0, pl.ds(0, feat)]),
                (down_hbm, down.at[0, pl.ds(0, feat)]),
            )
        )
    ]
    for load in loads:
        load.start()

    barrier = pltpu.get_barrier_semaphore()

    def greet(i, carry):
        e = lax.rem(g + i, experts)
        pl.semaphore_signal(barrier, inc=1, device_id=(d, e), device_id_type=MESH)
        pl.semaphore_signal(barrier, inc=1, device_id=(sib, e), device_id_type=MESH)
        return carry

    lax.fori_loop(1, experts, greet, 0)
    pl.semaphore_signal(barrier, inc=1, device_id=(sib, g), device_id_type=MESH)
    for i in range(1, chips):
        peer = lax.rem(y + i, chips) * 2 + c
        pl.semaphore_signal(barrier, inc=1, device_id=(peer, g), device_id_type=MESH)

    loads[0].wait()
    loads[1].wait()
    ids = ids_ref[...]
    probs = prob_ref[...].astype(F32)
    number = iota((128, block), 0)
    number_hi = iota((2 * HALF - feat, block), 0)
    named = jnp.zeros((128, block), F32)
    gates = jnp.zeros((2 * HALF - feat, block), F32)
    for k in range(top):
        line = ids[k : k + 1, :]
        named = named + jnp.where((line == number) & (number < experts), 1.0, 0.0)
        gates = gates + jnp.where(line == number_hi, probs[k : k + 1, :], 0.0)
    named = named.astype(BF16)
    earlier = jnp.where(iota((block, block), 0) < iota((block, block), 1), 1.0, 0.0).astype(BF16)
    before = dot(named, earlier).astype(BF16)
    spread = jnp.where(iota((rows, 128), 0) // CAP == iota((rows, 128), 1), 1.0, 0.0).astype(BF16)
    place = jnp.where(
        (dot(spread, named) > 0.5)
        & (dot(spread, before) == lax.rem(iota((rows, block), 0), CAP).astype(F32)),
        1.0,
        0.0,
    ).astype(BF16)
    held[...] = place

    def pack(low, hi, count):
        return jnp.concatenate(
            [low.reshape(count, CAP, HALF), hi.reshape(count, CAP, HALF)], axis=1
        ).astype(BF16)

    def unpack(message, count):
        wide = message.astype(F32)
        return (
            wide[:, :CAP].reshape(count * CAP, HALF),
            wide[:, CAP:].reshape(count * CAP, HALF),
        )

    loads[2].wait()
    tok_hi = jnp.concatenate([tok_ref[HALF:, :], gates.astype(BF16)], axis=0)
    send_x[...] = pack(dot(place, tok_ref[:HALF, :], 1, 1), dot(place, tok_hi, 1, 1), experts)
    loads[3].wait()
    cot_hi = jnp.concatenate([cot_ref[HALF:, :], jnp.zeros(gates.shape, BF16)], axis=0)
    send_dy[...] = pack(dot(place, cot_ref[:HALF, :], 1, 1), dot(place, cot_hi, 1, 1), experts)
    for s in range(2):
        up[s, feat:, :] = jnp.zeros((2 * HALF - feat, ff), BF16)
        down[s, feat:, :] = jnp.zeros((2 * HALF - feat, ff), BF16)

    pl.semaphore_wait(barrier, 2 * experts - 1 + chips - 1)

    def dispatch(source, target, n):
        def remote(e, core):
            return pltpu.make_async_remote_copy(
                src_ref=source.at[e],
                dst_ref=target.at[slot, place_of_mine],
                send_sem=send_sem.at[n],
                recv_sem=recv_sem.at[n],
                device_id=(core, e),
                device_id_type=MESH,
            )

        def body(i, carry):
            first = far_first(i) * ROW
            for turn in range(ROW):
                remote(first + lax.rem(x + turn, ROW), 2 * y + parity).start()
            return carry

        lax.fori_loop(0, rings - 1, body, 0)
        for turn in range(1, ROW):
            remote(z * ROW + lax.rem(x + turn, ROW), 2 * y + parity).start()

        @pl.when(c == parity)
        def _():
            pltpu.make_async_copy(source.at[g], target.at[0, place_of_mine], recv_sem.at[n]).start()

        @pl.when(c != parity)
        def _():
            remote(g, sib).start()

    def to_sibling(source, target, n):
        copy = pltpu.make_async_remote_copy(
            src_ref=source,
            dst_ref=target,
            send_sem=send_sem.at[n],
            recv_sem=recv_sem.at[n],
            device_id=(sib, g),
            device_id_type=MESH,
        )
        copy.start()
        return copy

    def arrived(buffer, n):
        pltpu.make_async_copy(buffer, buffer, recv_sem.at[n]).wait()

    def sent(buffer, n):
        pltpu.make_async_copy(buffer, buffer, send_sem.at[n]).wait()

    dispatch(send_x, got_x, 0)
    loads[4].wait()
    loads[5].wait()
    up_copy = to_sibling(up.at[0, pl.ds(0, feat)], up.at[1, pl.ds(0, feat)], 2)
    down_copy = to_sibling(down.at[0, pl.ds(0, feat)], down.at[1, pl.ds(0, feat)], 3)
    dispatch(send_dy, got_dy, 1)

    turns = [chips // 2]
    for i in range(1, (chips + 1) // 2):
        turns += [i, chips - i]

    def to_peers(source_of, target, n):
        for i in turns:
            peer = lax.rem(y + i, chips)
            pltpu.make_async_remote_copy(
                src_ref=source_of(peer),
                dst_ref=target,
                send_sem=send_sem.at[n],
                recv_sem=recv_sem.at[n],
                device_id=(peer * 2 + c, g),
                device_id_type=MESH,
            ).start()

    unit = ff // chips

    arrived(got_x, 0)
    low, hi = unpack(got_x[0], blocks)
    gate = jnp.sum(jnp.where(iota((half, HALF), 1) == g + high, hi, 0.0), axis=1, keepdims=True)
    rows_x[0] = jnp.concatenate([low, hi], axis=1).astype(BF16)
    low, hi = unpack(got_x[1], blocks)
    rows_x[2] = jnp.concatenate([low, hi], axis=1).astype(BF16)
    up_copy.wait()
    for n in range(ff // STEP):
        cols = pl.ds(n * STEP, STEP)
        product = dot(rows_x[0], up[0, :, cols]) + dot(rows_x[2], up[1, :, cols])
        for m in range(STEP // unit):
            piece = product[:, m * unit : (m + 1) * unit]
            own_h[n * (STEP // unit) + m] = piece
            part_h[n * (STEP // unit) + m] = piece.astype(BF16)
    to_peers(lambda peer: part_h.at[peer], sum_h.at[y], 4)
    x_copy = to_sibling(rows_x.at[2], rows_x.at[1], 5)

    arrived(got_dy, 1)
    for s in range(2):
        low, hi = unpack(got_dy[s], blocks)
        rows_dy[2 * s] = jnp.concatenate([low, hi], axis=1).astype(BF16)
    down_copy.wait()
    for n in range(ff // STEP):
        cols = pl.ds(n * STEP, STEP)
        product = dot(rows_dy[0], down[0, :, cols]) + dot(rows_dy[2], down[1, :, cols])
        for m in range(STEP // unit):
            piece = product[:, m * unit : (m + 1) * unit]
            own_q[n * (STEP // unit) + m] = piece
            part_q[n * (STEP // unit) + m] = piece.astype(BF16)
    to_peers(lambda peer: part_q.at[peer], sum_q.at[y], 6)
    dy_copy = to_sibling(rows_dy.at[2], rows_dy.at[1], 7)

    arrived(sum_h.at[pl.ds(0, chips - 1)], 4)
    hidden = own_h[y]
    for i in range(1, chips):
        hidden = hidden + sum_h[lax.rem(y + i, chips)].astype(F32)
    sigma = jax.nn.sigmoid(hidden)
    act = (hidden * sigma).astype(BF16).astype(F32)
    slope = gate * (sigma * (1.0 + hidden * (1.0 - sigma)))
    actg[0, y] = (gate * act).astype(BF16)
    arrived(sum_q.at[pl.ds(0, chips - 1)], 6)
    for p in range(2):
        span = pl.ds(p * part, part)
        query = own_q[y, span]
        for i in range(1, chips):
            query = query + sum_q[lax.rem(y + i, chips), span].astype(F32)
        here = slice(p * part, (p + 1) * part)
        hgrad[0, y, span] = (slope[here] * query).astype(BF16)
        to_peers(lambda peer: hgrad.at[0, y, span], hgrad.at[0, y, span], 8 + 6 * p)
        score[p, y] = lax.dot_general(
            jnp.ones((8, unit), F32),
            act[here] * query,
            (((1,), (1,)), ((), ())),
            precision=lax.Precision.HIGHEST,
            preferred_element_type=F32,
        )
        to_peers(lambda peer: score.at[p, y], score.at[p, y], 9 + 6 * p)

    mark = jnp.where(
        (iota((8, HALF), 0) == 0) & (iota((8, HALF), 1) == g + high), 1.0, 0.0
    ).astype(BF16)

    def remote_back(s, j, core, b):
        return pltpu.make_async_remote_copy(
            src_ref=ret.at[s, j],
            dst_ref=back.at[g],
            send_sem=send_sem.at[12],
            recv_sem=recv_sem.at[12],
            device_id=(core, b),
            device_id_type=MESH,
        )

    for p in range(2):
        span = pl.ds(p * part, part)
        arrived(hgrad.at[0, pl.ds(0, chips - 1), span], 8 + 6 * p)
        arrived(score.at[p, pl.ds(0, chips - 1)], 9 + 6 * p)
        total = score[p, 0]
        for i in range(1, chips):
            total = total + score[p, i]
        score_lane = dot(total.astype(BF16), mark, 0, 0)
        grad_rows = jnp.concatenate([hgrad[0, i, span] for i in range(chips)], axis=1)
        for s in range(2):
            low = dot(grad_rows, up[s, :HALF, :], 1, 1)
            hi = dot(grad_rows, up[s, HALF:, :], 1, 1) + score_lane
            ret[s, pl.ds(p * rings, rings)] = pack(low, hi, rings)
        column = 2 * p + c

        def body(i, carry, p=p, column=column):
            other = far_first(i)
            for s, core in ((0, d), (1, sib)):
                remote_back(s, p * rings + other, core, other * ROW + column).start()
            return carry

        lax.fori_loop(0, rings - 1, body, 0)
        remote_back(1, p * rings + z, sib, z * ROW + column).start()

        @pl.when(x == column)
        def _(p=p):
            pltpu.make_async_copy(ret.at[0, p * rings + z], back.at[g], recv_sem.at[12]).start()

        @pl.when(x != column)
        def _(p=p, column=column):
            remote_back(0, p * rings + z, d, z * ROW + column).start()

    hgrad_copy = to_sibling(hgrad.at[0], hgrad.at[1], 11)
    to_peers(lambda peer: actg.at[0, y], actg.at[0, y], 10)

    x_copy.wait()
    hgrad_copy.wait()
    own_x = jnp.concatenate([rows_x[0], rows_x[1]], axis=0)
    for n in range(ff // STEP):
        units = range(n * (STEP // unit), (n + 1) * (STEP // unit))
        right = jnp.concatenate(
            [jnp.concatenate([hgrad[0, i], hgrad[1, i]], axis=0) for i in units], axis=1
        )
        gup_ref[:, pl.ds(n * STEP, STEP)] = dot(own_x, right, 0, 0)[:feat].astype(BF16)
    arrived(actg.at[0, pl.ds(0, chips - 1)], 10)
    actg_copy = to_sibling(actg.at[0], actg.at[1], 13)
    dy_copy.wait()
    own_dy = jnp.concatenate([rows_dy[0], rows_dy[1]], axis=0)
    actg_copy.wait()
    for n in range(ff // STEP):
        units = range(n * (STEP // unit), (n + 1) * (STEP // unit))
        right = jnp.concatenate(
            [jnp.concatenate([actg[0, i], actg[1, i]], axis=0) for i in units], axis=1
        )
        gdown_ref[:, pl.ds(n * STEP, STEP)] = dot(own_dy, right, 0, 0)[:feat].astype(BF16)

    arrived(back, 12)
    low, hi = unpack(back[...], experts)
    gtok_ref[:HALF, :] = dot(low.astype(BF16), held[...], 0, 0).astype(BF16)
    summed = dot(hi.astype(BF16), held[...], 0, 0)
    gtok_ref[HALF:, :] = summed[:high].astype(BF16)
    found = jnp.zeros((top, block), F32)
    for k in range(top):
        value = jnp.sum(
            jnp.where(ids[k : k + 1, :] == number_hi, summed[high:], 0.0), axis=0, keepdims=True
        )
        found = found + jnp.where(iota((top, block), 0) == k, value, 0.0)
    gprob_ref[...] = found.astype(BF16)

    for n, buffer in ((0, send_x), (1, send_dy), (12, back)):

        @pl.when(c == parity)
        def _(n=n, buffer=buffer):
            sent(buffer.at[pl.ds(0, experts - 1)], n)

        @pl.when(c != parity)
        def _(n=n, buffer=buffer):
            sent(buffer, n)

    for n, buffer in ((4, sum_h), (6, sum_q), (10, actg.at[0])):
        sent(buffer.at[pl.ds(0, chips - 1)], n)
    for p in range(2):
        sent(hgrad.at[0, pl.ds(0, chips - 1), pl.ds(p * part, part)], 8 + 6 * p)
        sent(score.at[p, pl.ds(0, chips - 1)], 9 + 6 * p)


def hand_over(*refs):
    count = len(refs) // 2
    sem = refs[-1]
    copies = [pltpu.make_async_copy(refs[n], refs[count + n], sem.at[n]) for n in range(count)]
    for copy in copies:
        copy.start()
    for copy in copies:
        copy.wait()


def on_device(tokens, cotangent, expert_ids, route_probs, w_up, w_down):
    experts = lax.axis_size("expert")
    chips = lax.axis_size("dp") // 2
    block, feat = tokens.shape
    top = expert_ids.shape[1]
    ff = w_up.shape[2]
    half = experts * CAP // 2
    blocks = experts // 2
    unit = ff // chips
    wide = 2 * HALF
    vmem = pl.BlockSpec(memory_space=pltpu.VMEM)
    anywhere = pl.BlockSpec(memory_space=pl.ANY)
    results = pl.pallas_call(
        functools.partial(kernel, experts, chips),
        out_shape=(
            jax.ShapeDtypeStruct((feat, block), BF16),
            jax.ShapeDtypeStruct((top, block), BF16),
            jax.ShapeDtypeStruct((feat, ff), BF16),
            jax.ShapeDtypeStruct((feat, ff), BF16),
        ),
        in_specs=[anywhere] * 6,
        out_specs=[vmem] * 4,
        scratch_shapes=[
            pltpu.VMEM((feat, block), BF16),
            pltpu.VMEM((feat, block), BF16),
            pltpu.VMEM((top, block), jnp.int32),
            pltpu.VMEM((top, block), BF16),
            pltpu.VMEM((experts, MSG, HALF), BF16),
            pltpu.VMEM((experts, MSG, HALF), BF16),
            pltpu.VMEM((2, blocks, MSG, HALF), BF16),
            pltpu.VMEM((2, blocks, MSG, HALF), BF16),
            pltpu.VMEM((2, wide, ff), BF16),
            pltpu.VMEM((2, wide, ff), BF16),
            pltpu.VMEM((3, half, wide), BF16),
            pltpu.VMEM((3, half, wide), BF16),
            pltpu.VMEM((chips, half, unit), BF16),
            pltpu.VMEM((chips, half, unit), BF16),
            pltpu.VMEM((chips, half, unit), F32),
            pltpu.VMEM((chips, half, unit), F32),
            pltpu.VMEM((chips, half, unit), BF16),
            pltpu.VMEM((chips, half, unit), BF16),
            pltpu.VMEM((2, chips, half, unit), BF16),
            pltpu.VMEM((2, chips, half, unit), BF16),
            pltpu.VMEM((2, chips, 8, half // 2), F32),
            pltpu.VMEM((2, blocks, MSG, HALF), BF16),
            pltpu.VMEM((experts, MSG, HALF), BF16),
            pltpu.VMEM((experts * CAP, block), BF16),
            pltpu.SemaphoreType.DMA((6,)),
            pltpu.SemaphoreType.DMA((16,)),
            pltpu.SemaphoreType.DMA((16,)),
        ],
        compiler_params=pltpu.CompilerParams(
            collective_id=0, has_side_effects=True, vmem_limit_bytes=56 * 2**20
        ),
        name="expert_backward",
    )(tokens.T, cotangent.T, expert_ids.T, route_probs.T, w_up[0], w_down[0].T)
    grad_tokens, grad_probs, grad_up, grad_down = pl.pallas_call(
        hand_over,
        out_shape=tuple(jax.ShapeDtypeStruct(r.shape, r.dtype) for r in results),
        in_specs=[anywhere] * 4,
        out_specs=[anywhere] * 4,
        scratch_shapes=[pltpu.SemaphoreType.DMA((4,))],
        name="hand_over",
    )(*results)
    return (grad_tokens.T, grad_probs.T, grad_up[None], grad_down.T[None])


def solution(mesh):
    in_specs = (
        P("expert", "dp"),
        P("expert", "dp"),
        P("expert", None),
        P("expert", None),
        P("expert", "dp", None),
        P("expert", None, "dp"),
    )
    out_specs = (
        P("expert", "dp"),
        P("expert", None),
        P("expert", "dp", None),
        P("expert", None, "dp"),
    )
    return jax.shard_map(
        on_device, mesh=mesh, in_specs=in_specs, out_specs=out_specs, check_vma=False
    )
```

```python
import functools

import jax
import jax.numpy as jnp
from jax import lax
from jax.experimental import pallas as pl
from jax.experimental.pallas import tpu as pltpu
from jax.sharding import PartitionSpec as P

CAP = 8
MSG = 16
HALF = 256
STEP = 256
ROW = 4
MESH = pl.DeviceIdType.MESH
BF16, F32 = jnp.bfloat16, jnp.float32


def dot(left, right, left_dim=1, right_dim=0):
    return lax.dot_general(
        left, right, (((left_dim,), (right_dim,)), ((), ())), preferred_element_type=F32
    )


def iota(shape, dim):
    return lax.broadcasted_iota(jnp.int32, shape, dim)


def kernel(
    experts,
    chips,
    tok_hbm,
    cot_hbm,
    ids_hbm,
    prob_hbm,
    up_hbm,
    down_hbm,
    gtok_ref,
    gprob_ref,
    gup_hbm,
    gdown_hbm,
    tok_ref,
    cot_ref,
    ids_ref,
    prob_ref,
    send_x,
    send_dy,
    got_x,
    got_dy,
    up,
    down,
    rows_x,
    rows_dy,
    part_h,
    part_q,
    own_h,
    own_q,
    sum_h,
    sum_q,
    hgrad,
    actg,
    score,
    ret,
    back,
    held,
    gup_ref,
    gdown_ref,
    load_sem,
    send_sem,
    recv_sem,
):
    d = lax.axis_index("dp")
    g = lax.axis_index("expert")
    y, c = d // 2, lax.rem(d, 2)
    sib = 2 * y + 1 - c
    parity = lax.rem(g, 2)
    slot = lax.rem(c + parity, 2)
    feat, block = tok_hbm.shape
    top = ids_hbm.shape[0]
    ff = up_hbm.shape[1]
    rows = experts * CAP
    half = rows // 2
    blocks = experts // 2
    high = feat - HALF
    rings = experts // ROW
    z, x = g // ROW, lax.rem(g, ROW)
    part = half // 2
    place_of_mine = (x // 2) * rings + z

    def far_first(i):
        j = rings - 1 - i
        near = (j + 1) // 2
        return lax.rem(z + jnp.where(lax.rem(j, 2) == 1, near, rings - near), rings)

    loads = [
        pltpu.make_async_copy(source, target, load_sem.at[n])
        for n, (source, target) in enumerate(
            (
                (ids_hbm, ids_ref),
                (prob_hbm, prob_ref),
                (tok_hbm, tok_ref),
                (cot_hbm, cot_ref),
                (up_hbm, up.at[0, pl.ds(0, feat)]),
                (down_hbm, down.at[0, pl.ds(0, feat)]),
            )
        )
    ]
    for load in loads:
        load.start()

    barrier = pltpu.get_barrier_semaphore()

    def greet(i, carry):
        e = lax.rem(g + i, experts)
        pl.semaphore_signal(barrier, inc=1, device_id=(d, e), device_id_type=MESH)
        pl.semaphore_signal(barrier, inc=1, device_id=(sib, e), device_id_type=MESH)
        return carry

    lax.fori_loop(1, experts, greet, 0)
    pl.semaphore_signal(barrier, inc=1, device_id=(sib, g), device_id_type=MESH)
    for i in range(1, chips):
        peer = lax.rem(y + i, chips) * 2 + c
        pl.semaphore_signal(barrier, inc=1, device_id=(peer, g), device_id_type=MESH)

    loads[0].wait()
    loads[1].wait()
    ids = ids_ref[...]
    probs = prob_ref[...].astype(F32)
    number = iota((128, block), 0)
    number_hi = iota((2 * HALF - feat, block), 0)
    named = jnp.zeros((128, block), F32)
    gates = jnp.zeros((2 * HALF - feat, block), F32)
    for k in range(top):
        line = ids[k : k + 1, :]
        named = named + jnp.where((line == number) & (number < experts), 1.0, 0.0)
        gates = gates + jnp.where(line == number_hi, probs[k : k + 1, :], 0.0)
    named = named.astype(BF16)
    earlier = jnp.where(iota((block, block), 0) < iota((block, block), 1), 1.0, 0.0).astype(BF16)
    before = dot(named, earlier).astype(BF16)
    spread = jnp.where(iota((rows, 128), 0) // CAP == iota((rows, 128), 1), 1.0, 0.0).astype(BF16)
    place = jnp.where(
        (dot(spread, named) > 0.5)
        & (dot(spread, before) == lax.rem(iota((rows, block), 0), CAP).astype(F32)),
        1.0,
        0.0,
    ).astype(BF16)
    held[...] = place

    def pack(low, hi, count):
        return jnp.concatenate(
            [low.reshape(count, CAP, HALF), hi.reshape(count, CAP, HALF)], axis=1
        ).astype(BF16)

    def unpack(message, count):
        wide = message.astype(F32)
        return (
            wide[:, :CAP].reshape(count * CAP, HALF),
            wide[:, CAP:].reshape(count * CAP, HALF),
        )

    loads[2].wait()
    tok_hi = jnp.concatenate([tok_ref[HALF:, :], gates.astype(BF16)], axis=0)
    send_x[...] = pack(dot(place, tok_ref[:HALF, :], 1, 1), dot(place, tok_hi, 1, 1), experts)
    loads[3].wait()
    cot_hi = jnp.concatenate([cot_ref[HALF:, :], jnp.zeros(gates.shape, BF16)], axis=0)
    send_dy[...] = pack(dot(place, cot_ref[:HALF, :], 1, 1), dot(place, cot_hi, 1, 1), experts)
    for s in range(2):
        up[s, feat:, :] = jnp.zeros((2 * HALF - feat, ff), BF16)
        down[s, feat:, :] = jnp.zeros((2 * HALF - feat, ff), BF16)

    pl.semaphore_wait(barrier, 2 * experts - 1 + chips - 1)

    def dispatch(source, target, n):
        def remote(e, core):
            return pltpu.make_async_remote_copy(
                src_ref=source.at[e],
                dst_ref=target.at[slot, place_of_mine],
                send_sem=send_sem.at[n],
                recv_sem=recv_sem.at[n],
                device_id=(core, e),
                device_id_type=MESH,
            )

        def body(i, carry):
            first = far_first(i) * ROW
            for turn in range(ROW):
                remote(first + lax.rem(x + turn, ROW), 2 * y + parity).start()
            return carry

        lax.fori_loop(0, rings - 1, body, 0)
        for turn in range(1, ROW):
            remote(z * ROW + lax.rem(x + turn, ROW), 2 * y + parity).start()

        @pl.when(c == parity)
        def _():
            pltpu.make_async_copy(source.at[g], target.at[0, place_of_mine], recv_sem.at[n]).start()

        @pl.when(c != parity)
        def _():
            remote(g, sib).start()

    def to_sibling(source, target, n):
        copy = pltpu.make_async_remote_copy(
            src_ref=source,
            dst_ref=target,
            send_sem=send_sem.at[n],
            recv_sem=recv_sem.at[n],
            device_id=(sib, g),
            device_id_type=MESH,
        )
        copy.start()
        return copy

    def arrived(buffer, n):
        pltpu.make_async_copy(buffer, buffer, recv_sem.at[n]).wait()

    def sent(buffer, n):
        pltpu.make_async_copy(buffer, buffer, send_sem.at[n]).wait()

    dispatch(send_x, got_x, 0)
    loads[4].wait()
    loads[5].wait()
    up_copy = to_sibling(up.at[0, pl.ds(0, feat)], up.at[1, pl.ds(0, feat)], 2)
    down_copy = to_sibling(down.at[0, pl.ds(0, feat)], down.at[1, pl.ds(0, feat)], 3)
    dispatch(send_dy, got_dy, 1)

    turns = [chips // 2]
    for i in range(1, (chips + 1) // 2):
        turns += [i, chips - i]

    def to_peers(source_of, target, n):
        for i in turns:
            peer = lax.rem(y + i, chips)
            pltpu.make_async_remote_copy(
                src_ref=source_of(peer),
                dst_ref=target,
                send_sem=send_sem.at[n],
                recv_sem=recv_sem.at[n],
                device_id=(peer * 2 + c, g),
                device_id_type=MESH,
            ).start()

    unit = ff // chips

    arrived(got_x, 0)
    low, hi = unpack(got_x[0], blocks)
    gate = jnp.sum(jnp.where(iota((half, HALF), 1) == g + high, hi, 0.0), axis=1, keepdims=True)
    rows_x[0] = jnp.concatenate([low, hi], axis=1).astype(BF16)
    low, hi = unpack(got_x[1], blocks)
    rows_x[2] = jnp.concatenate([low, hi], axis=1).astype(BF16)
    up_copy.wait()
    for n in range(ff // STEP):
        cols = pl.ds(n * STEP, STEP)
        product = dot(rows_x[0], up[0, :, cols]) + dot(rows_x[2], up[1, :, cols])
        for m in range(STEP // unit):
            piece = product[:, m * unit : (m + 1) * unit]
            own_h[n * (STEP // unit) + m] = piece
            part_h[n * (STEP // unit) + m] = piece.astype(BF16)
    to_peers(lambda peer: part_h.at[peer], sum_h.at[y], 4)
    x_copy = to_sibling(rows_x.at[2], rows_x.at[1], 5)

    arrived(got_dy, 1)
    for s in range(2):
        low, hi = unpack(got_dy[s], blocks)
        rows_dy[2 * s] = jnp.concatenate([low, hi], axis=1).astype(BF16)
    down_copy.wait()
    for n in range(ff // STEP):
        cols = pl.ds(n * STEP, STEP)
        product = dot(rows_dy[0], down[0, :, cols]) + dot(rows_dy[2], down[1, :, cols])
        for m in range(STEP // unit):
            piece = product[:, m * unit : (m + 1) * unit]
            own_q[n * (STEP // unit) + m] = piece
            part_q[n * (STEP // unit) + m] = piece.astype(BF16)
    to_peers(lambda peer: part_q.at[peer], sum_q.at[y], 6)
    dy_copy = to_sibling(rows_dy.at[2], rows_dy.at[1], 7)

    arrived(sum_h.at[pl.ds(0, chips - 1)], 4)
    hidden = own_h[y]
    for i in range(1, chips):
        hidden = hidden + sum_h[lax.rem(y + i, chips)].astype(F32)
    sigma = jax.nn.sigmoid(hidden)
    act = (hidden * sigma).astype(BF16).astype(F32)
    slope = gate * (sigma * (1.0 + hidden * (1.0 - sigma)))
    actg[0, y] = (gate * act).astype(BF16)
    arrived(sum_q.at[pl.ds(0, chips - 1)], 6)
    for p in range(2):
        span = pl.ds(p * part, part)
        query = own_q[y, span]
        for i in range(1, chips):
            query = query + sum_q[lax.rem(y + i, chips), span].astype(F32)
        here = slice(p * part, (p + 1) * part)
        hgrad[0, y, span] = (slope[here] * query).astype(BF16)
        to_peers(lambda peer: hgrad.at[0, y, span], hgrad.at[0, y, span], 8 + 6 * p)
        score[p, y] = lax.dot_general(
            jnp.ones((8, unit), F32),
            act[here] * query,
            (((1,), (1,)), ((), ())),
            precision=lax.Precision.HIGHEST,
            preferred_element_type=F32,
        )
        to_peers(lambda peer: score.at[p, y], score.at[p, y], 9 + 6 * p)

    mark = jnp.where(
        (iota((8, HALF), 0) == 0) & (iota((8, HALF), 1) == g + high), 1.0, 0.0
    ).astype(BF16)

    def remote_back(s, j, core, b):
        return pltpu.make_async_remote_copy(
            src_ref=ret.at[s, j],
            dst_ref=back.at[g],
            send_sem=send_sem.at[12],
            recv_sem=recv_sem.at[12],
            device_id=(core, b),
            device_id_type=MESH,
        )

    for p in range(2):
        span = pl.ds(p * part, part)
        arrived(hgrad.at[0, pl.ds(0, chips - 1), span], 8 + 6 * p)
        arrived(score.at[p, pl.ds(0, chips - 1)], 9 + 6 * p)
        total = score[p, 0]
        for i in range(1, chips):
            total = total + score[p, i]
        score_lane = dot(total.astype(BF16), mark, 0, 0)
        grad_rows = jnp.concatenate([hgrad[0, i, span] for i in range(chips)], axis=1)
        for s in range(2):
            low = dot(grad_rows, up[s, :HALF, :], 1, 1)
            hi = dot(grad_rows, up[s, HALF:, :], 1, 1) + score_lane
            ret[s, pl.ds(p * rings, rings)] = pack(low, hi, rings)
        column = 2 * p + c

        def body(i, carry, p=p, column=column):
            other = far_first(i)
            for s, core in ((0, d), (1, sib)):
                remote_back(s, p * rings + other, core, other * ROW + column).start()
            return carry

        lax.fori_loop(0, rings - 1, body, 0)
        remote_back(1, p * rings + z, sib, z * ROW + column).start()

        @pl.when(x == column)
        def _(p=p):
            pltpu.make_async_copy(ret.at[0, p * rings + z], back.at[g], recv_sem.at[12]).start()

        @pl.when(x != column)
        def _(p=p, column=column):
            remote_back(0, p * rings + z, d, z * ROW + column).start()

    hgrad_copy = to_sibling(hgrad.at[0], hgrad.at[1], 11)
    to_peers(lambda peer: actg.at[0, y], actg.at[0, y], 10)

    x_copy.wait()
    hgrad_copy.wait()
    own_x = jnp.concatenate([rows_x[0], rows_x[1]], axis=0)
    for n in range(ff // STEP):
        units = range(n * (STEP // unit), (n + 1) * (STEP // unit))
        right = jnp.concatenate(
            [jnp.concatenate([hgrad[0, i], hgrad[1, i]], axis=0) for i in units], axis=1
        )
        gup_ref[:, pl.ds(n * STEP, STEP)] = dot(own_x, right, 0, 0)[:feat].astype(BF16)
    gup_copy = pltpu.make_async_copy(gup_ref, gup_hbm, load_sem.at[6])
    gup_copy.start()
    arrived(actg.at[0, pl.ds(0, chips - 1)], 10)
    actg_copy = to_sibling(actg.at[0], actg.at[1], 13)
    dy_copy.wait()
    own_dy = jnp.concatenate([rows_dy[0], rows_dy[1]], axis=0)
    actg_copy.wait()
    for n in range(ff // STEP):
        units = range(n * (STEP // unit), (n + 1) * (STEP // unit))
        right = jnp.concatenate(
            [jnp.concatenate([actg[0, i], actg[1, i]], axis=0) for i in units], axis=1
        )
        gdown_ref[:, pl.ds(n * STEP, STEP)] = dot(own_dy, right, 0, 0)[:feat].astype(BF16)

    gdown_copy = pltpu.make_async_copy(gdown_ref, gdown_hbm, load_sem.at[7])
    gdown_copy.start()

    arrived(back, 12)
    low, hi = unpack(back[...], experts)
    gtok_ref[:HALF, :] = dot(low.astype(BF16), held[...], 0, 0).astype(BF16)
    summed = dot(hi.astype(BF16), held[...], 0, 0)
    gtok_ref[HALF:, :] = summed[:high].astype(BF16)
    found = jnp.zeros((top, block), F32)
    for k in range(top):
        value = jnp.sum(
            jnp.where(ids[k : k + 1, :] == number_hi, summed[high:], 0.0), axis=0, keepdims=True
        )
        found = found + jnp.where(iota((top, block), 0) == k, value, 0.0)
    gprob_ref[...] = found.astype(BF16)

    gup_copy.wait()
    gdown_copy.wait()
    for n, buffer in ((0, send_x), (1, send_dy), (12, back)):

        @pl.when(c == parity)
        def _(n=n, buffer=buffer):
            sent(buffer.at[pl.ds(0, experts - 1)], n)

        @pl.when(c != parity)
        def _(n=n, buffer=buffer):
            sent(buffer, n)

    for n, buffer in ((4, sum_h), (6, sum_q), (10, actg.at[0])):
        sent(buffer.at[pl.ds(0, chips - 1)], n)
    for p in range(2):
        sent(hgrad.at[0, pl.ds(0, chips - 1), pl.ds(p * part, part)], 8 + 6 * p)
        sent(score.at[p, pl.ds(0, chips - 1)], 9 + 6 * p)


def hand_over(*refs):
    count = len(refs) // 3
    source, target, middle = refs[:count], refs[count : 2 * count], refs[2 * count : 3 * count]
    sem = refs[-1]
    loads = [pltpu.make_async_copy(source[n], middle[n], sem.at[0, n]) for n in range(count)]
    stores = [pltpu.make_async_copy(middle[n], target[n], sem.at[1, n]) for n in range(count)]
    for load in loads:
        load.start()
    for load, store in zip(loads, stores):
        load.wait()
        store.start()
    for store in stores:
        store.wait()


def on_device(tokens, cotangent, expert_ids, route_probs, w_up, w_down):
    experts = lax.axis_size("expert")
    chips = lax.axis_size("dp") // 2
    block, feat = tokens.shape
    top = expert_ids.shape[1]
    ff = w_up.shape[2]
    half = experts * CAP // 2
    blocks = experts // 2
    unit = ff // chips
    wide = 2 * HALF
    vmem = pl.BlockSpec(memory_space=pltpu.VMEM)
    anywhere = pl.BlockSpec(memory_space=pl.ANY)
    results = pl.pallas_call(
        functools.partial(kernel, experts, chips),
        out_shape=(
            jax.ShapeDtypeStruct((feat, block), BF16),
            jax.ShapeDtypeStruct((top, block), BF16),
            jax.ShapeDtypeStruct((feat, ff), BF16),
            jax.ShapeDtypeStruct((feat, ff), BF16),
        ),
        in_specs=[anywhere] * 6,
        out_specs=[vmem] * 2 + [anywhere] * 2,
        scratch_shapes=[
            pltpu.VMEM((feat, block), BF16),
            pltpu.VMEM((feat, block), BF16),
            pltpu.VMEM((top, block), jnp.int32),
            pltpu.VMEM((top, block), BF16),
            pltpu.VMEM((experts, MSG, HALF), BF16),
            pltpu.VMEM((experts, MSG, HALF), BF16),
            pltpu.VMEM((2, blocks, MSG, HALF), BF16),
            pltpu.VMEM((2, blocks, MSG, HALF), BF16),
            pltpu.VMEM((2, wide, ff), BF16),
            pltpu.VMEM((2, wide, ff), BF16),
            pltpu.VMEM((3, half, wide), BF16),
            pltpu.VMEM((3, half, wide), BF16),
            pltpu.VMEM((chips, half, unit), BF16),
            pltpu.VMEM((chips, half, unit), BF16),
            pltpu.VMEM((chips, half, unit), F32),
            pltpu.VMEM((chips, half, unit), F32),
            pltpu.VMEM((chips, half, unit), BF16),
            pltpu.VMEM((chips, half, unit), BF16),
            pltpu.VMEM((2, chips, half, unit), BF16),
            pltpu.VMEM((2, chips, half, unit), BF16),
            pltpu.VMEM((2, chips, 8, half // 2), F32),
            pltpu.VMEM((2, blocks, MSG, HALF), BF16),
            pltpu.VMEM((experts, MSG, HALF), BF16),
            pltpu.VMEM((experts * CAP, block), BF16),
            pltpu.VMEM((feat, ff), BF16),
            pltpu.VMEM((feat, ff), BF16),
            pltpu.SemaphoreType.DMA((8,)),
            pltpu.SemaphoreType.DMA((16,)),
            pltpu.SemaphoreType.DMA((16,)),
        ],
        compiler_params=pltpu.CompilerParams(
            collective_id=0, has_side_effects=True, vmem_limit_bytes=56 * 2**20
        ),
        name="expert_backward",
    )(tokens.T, cotangent.T, expert_ids.T, route_probs.T, w_up[0], w_down[0].T)
    grad_tokens, grad_probs, grad_up, grad_down = pl.pallas_call(
        hand_over,
        out_shape=tuple(jax.ShapeDtypeStruct(r.shape, r.dtype) for r in results),
        in_specs=[anywhere] * 4,
        out_specs=[anywhere] * 4,
        scratch_shapes=[pltpu.VMEM(r.shape, r.dtype) for r in results] + [pltpu.SemaphoreType.DMA((2, 4))],
        name="hand_over",
    )(*results)
    return (grad_tokens.T, grad_probs.T, grad_up[None], grad_down.T[None])


def solution(mesh):
    in_specs = (
        P("expert", "dp"),
        P("expert", "dp"),
        P("expert", None),
        P("expert", None),
        P("expert", "dp", None),
        P("expert", None, "dp"),
    )
    out_specs = (
        P("expert", "dp"),
        P("expert", None),
        P("expert", "dp", None),
        P("expert", None, "dp"),
    )
    return jax.shard_map(
        on_device, mesh=mesh, in_specs=in_specs, out_specs=out_specs, check_vma=False
    )
```

```python
import functools

import jax
import jax.numpy as jnp
from jax import lax
from jax.experimental import pallas as pl
from jax.experimental.pallas import tpu as pltpu
from jax.sharding import PartitionSpec as P

CAP = 8
PARTS = 2
SUB = CAP // PARTS
FIELDS = 4
MSG = FIELDS * SUB
HALF = 256
QUARTER = 128
STEP = 256
ROW = 4
MESH = pl.DeviceIdType.MESH
BF16, F32 = jnp.bfloat16, jnp.float32


def dot(left, right, left_dim=1, right_dim=0):
    return lax.dot_general(
        left, right, (((left_dim,), (right_dim,)), ((), ())), preferred_element_type=F32
    )


def iota(shape, dim):
    return lax.broadcasted_iota(jnp.int32, shape, dim)


def kernel(
    experts,
    chips,
    tok_hbm,
    cot_hbm,
    ids_hbm,
    prob_hbm,
    up_hbm,
    down_hbm,
    gtok_ref,
    gprob_ref,
    gup_hbm,
    gdown_hbm,
    tok_ref,
    cot_ref,
    ids_ref,
    prob_ref,
    send,
    got,
    up,
    down,
    rows_x,
    rows_dy,
    part,
    own,
    sums,
    hgrad,
    actg,
    score,
    ret,
    back,
    placed,
    combined,
    gup_ref,
    gdown_ref,
    load_sem,
    send_sem,
    recv_sem,
):
    d = lax.axis_index("dp")
    g = lax.axis_index("expert")
    y, c = d // 2, lax.rem(d, 2)
    sib = 2 * y + 1 - c
    parity = lax.rem(g, 2)
    slot = lax.rem(c + parity, 2)
    feat, block = tok_hbm.shape
    top = ids_hbm.shape[0]
    ff = up_hbm.shape[1]
    blocks = experts // 2
    count = blocks * SUB
    high = feat - HALF
    rings = experts // ROW
    z, x = g // ROW, lax.rem(g, ROW)

    def far_first(i):
        j = rings - 1 - i
        near = (j + 1) // 2
        return lax.rem(z + jnp.where(lax.rem(j, 2) == 1, near, rings - near), rings)

    loads = [
        pltpu.make_async_copy(source, target, load_sem.at[n])
        for n, (source, target) in enumerate(
            (
                (ids_hbm, ids_ref),
                (prob_hbm, prob_ref),
                (tok_hbm, tok_ref),
                (cot_hbm, cot_ref),
                (up_hbm, up.at[0, pl.ds(0, feat)]),
                (down_hbm, down.at[0, pl.ds(0, feat)]),
            )
        )
    ]
    for load in loads:
        load.start()

    barrier = pltpu.get_barrier_semaphore()

    def greet(i, carry):
        e = lax.rem(g + i, experts)
        pl.semaphore_signal(barrier, inc=1, device_id=(d, e), device_id_type=MESH)
        pl.semaphore_signal(barrier, inc=1, device_id=(sib, e), device_id_type=MESH)
        return carry

    lax.fori_loop(1, experts, greet, 0)
    pl.semaphore_signal(barrier, inc=1, device_id=(sib, g), device_id_type=MESH)
    for i in range(1, chips):
        peer = lax.rem(y + i, chips) * 2 + c
        pl.semaphore_signal(barrier, inc=1, device_id=(peer, g), device_id_type=MESH)

    loads[0].wait()
    loads[1].wait()
    ids = ids_ref[...]
    probs = prob_ref[...].astype(F32)
    number = iota((128, block), 0)
    number_hi = iota((2 * HALF - feat, block), 0)
    named = jnp.zeros((128, block), F32)
    gates = jnp.zeros((2 * HALF - feat, block), F32)
    for k in range(top):
        line = ids[k : k + 1, :]
        named = named + jnp.where((line == number) & (number < experts), 1.0, 0.0)
        gates = gates + jnp.where(line == number_hi, probs[k : k + 1, :], 0.0)
    named = named.astype(BF16)
    earlier = jnp.where(iota((block, block), 0) < iota((block, block), 1), 1.0, 0.0).astype(BF16)
    before = dot(named, earlier).astype(BF16)
    lines = experts * MSG
    spread = jnp.where(iota((lines, 128), 0) // MSG == iota((lines, 128), 1), 1.0, 0.0).astype(BF16)
    named_line = dot(spread, named)
    rank_line = dot(spread, before)
    rank = lax.rem(iota((lines, block), 0), SUB)
    field = lax.rem(iota((lines, block), 0) // SUB, FIELDS)
    for k in range(PARTS):
        fills = (named_line > 0.5) & (rank_line == (rank + k * SUB).astype(F32))
        for q in range(FIELDS):
            placed[k, :, q * block : (q + 1) * block] = jnp.where(
                fills & (field == q), 1.0, 0.0
            ).astype(BF16)

    loads[2].wait()
    loads[3].wait()
    source = jnp.concatenate(
        [
            tok_ref[:HALF, :],
            jnp.concatenate([tok_ref[HALF:, :], gates.astype(BF16)], axis=0),
            cot_ref[:HALF, :],
            jnp.concatenate([cot_ref[HALF:, :], jnp.zeros(gates.shape, BF16)], axis=0),
        ],
        axis=1,
    )

    def fill(k):
        send[k] = dot(placed[k], source, 1, 1).astype(BF16).reshape(experts, MSG, HALF)

    fill(0)
    for s in range(2):
        up[s, feat:, :] = jnp.zeros((2 * HALF - feat, ff), BF16)
        down[s, feat:, :] = jnp.zeros((2 * HALF - feat, ff), BF16)

    pl.semaphore_wait(barrier, 2 * experts - 1 + chips - 1)

    def dispatch(n):
        def remote(e, core):
            return pltpu.make_async_remote_copy(
                src_ref=send.at[n, e],
                dst_ref=got.at[n, slot, g // 2],
                send_sem=send_sem.at[n],
                recv_sem=recv_sem.at[n],
                device_id=(core, e),
                device_id_type=MESH,
            )

        def body(i, carry):
            first = far_first(i) * ROW
            for turn in range(ROW):
                remote(first + lax.rem(x + turn, ROW), 2 * y + parity).start()
            return carry

        lax.fori_loop(0, rings - 1, body, 0)
        for turn in range(1, ROW):
            remote(z * ROW + lax.rem(x + turn, ROW), 2 * y + parity).start()

        @pl.when(c == parity)
        def _():
            pltpu.make_async_copy(send.at[n, g], got.at[n, 0, g // 2], recv_sem.at[n]).start()

        @pl.when(c != parity)
        def _():
            remote(g, sib).start()

    def to_sibling(source, target, n):
        copy = pltpu.make_async_remote_copy(
            src_ref=source,
            dst_ref=target,
            send_sem=send_sem.at[n],
            recv_sem=recv_sem.at[n],
            device_id=(sib, g),
            device_id_type=MESH,
        )
        copy.start()
        return copy

    def arrived(buffer, n):
        pltpu.make_async_copy(buffer, buffer, recv_sem.at[n]).wait()

    def sent(buffer, n):
        pltpu.make_async_copy(buffer, buffer, send_sem.at[n]).wait()

    dispatch(0)
    loads[4].wait()
    loads[5].wait()
    up_copy = to_sibling(up.at[0, pl.ds(0, feat)], up.at[1, pl.ds(0, feat)], 2)
    down_copy = to_sibling(down.at[0, pl.ds(0, feat)], down.at[1, pl.ds(0, feat)], 3)
    fill(1)
    dispatch(1)

    turns = [chips // 2]
    for i in range(1, (chips + 1) // 2):
        turns += [i, chips - i]

    def to_peers(source_of, target, n):
        for i in turns:
            peer = lax.rem(y + i, chips)
            pltpu.make_async_remote_copy(
                src_ref=source_of(peer),
                dst_ref=target,
                send_sem=send_sem.at[n],
                recv_sem=recv_sem.at[n],
                device_id=(peer * 2 + c, g),
                device_id_type=MESH,
            ).start()

    unit = ff // chips

    i = iota((count, blocks * MSG), 0)
    line = (i // SUB) * MSG + lax.rem(i, SUB) - iota((count, blocks * MSG), 1)
    take = jnp.concatenate(
        [jnp.where(line == -q * SUB, 1.0, 0.0).astype(BF16) for q in range(FIELDS)], axis=0
    )

    def received(k):
        arrived(got.at[k], k)
        for s in range(2):
            fields = dot(take, got[k, s].reshape(blocks * MSG, HALF))
            low, hi, dlow, dhi = (fields[q * count : (q + 1) * count] for q in range(FIELDS))
            rows_x[k, 2 * s] = jnp.concatenate([low, hi], axis=1).astype(BF16)
            rows_dy[k, 2 * s] = jnp.concatenate([dlow, dhi], axis=1).astype(BF16)
            if s == 0:
                lane = iota((count, HALF), 1)
                gate = jnp.sum(jnp.where(lane == g + high, hi, 0.0), axis=1, keepdims=True)
        if k == 0:
            up_copy.wait()
            down_copy.wait()
        for n in range(ff // STEP):
            cols = pl.ds(n * STEP, STEP)
            product = jnp.concatenate(
                [
                    dot(rows_x[k, 0], up[0, :, cols]) + dot(rows_x[k, 2], up[1, :, cols]),
                    dot(rows_dy[k, 0], down[0, :, cols]) + dot(rows_dy[k, 2], down[1, :, cols]),
                ],
                axis=0,
            )
            for m in range(STEP // unit):
                piece = product[:, m * unit : (m + 1) * unit]
                own[k, n * (STEP // unit) + m] = piece
                part[k, n * (STEP // unit) + m] = piece.astype(BF16)
        to_peers(lambda peer: part.at[k, peer], sums.at[k, y], 4 + k)
        x_copy = to_sibling(rows_x.at[k, 2], rows_x.at[k, 1], 12 + k)
        dy_copy = to_sibling(rows_dy.at[k, 2], rows_dy.at[k, 1], 14 + k)
        return gate, x_copy, dy_copy

    def activate(k, gate):
        arrived(sums.at[k, pl.ds(0, chips - 1)], 4 + k)
        total = own[k, y]
        for i in range(1, chips):
            total = total + sums[k, lax.rem(y + i, chips)].astype(F32)
        hidden, query = total[:count], total[count:]
        sigma = jax.nn.sigmoid(hidden)
        hgrad[k, 0, y] = (gate * query * (sigma * (1.0 + hidden * (1.0 - sigma)))).astype(BF16)
        to_peers(lambda peer: hgrad.at[k, 0, y], hgrad.at[k, 0, y], 6 + k)
        act = (hidden * sigma).astype(BF16).astype(F32)
        score[k, y] = lax.dot_general(
            jnp.ones((8, unit), F32),
            act * query,
            (((1,), (1,)), ((), ())),
            precision=lax.Precision.HIGHEST,
            preferred_element_type=F32,
        )
        to_peers(lambda peer: score.at[k, y], score.at[k, y], 8 + k)
        actg[k, 0, y] = (gate * act).astype(BF16)

    def share_act(k):
        to_peers(lambda peer: actg.at[k, 0, y], actg.at[k, 0, y], 10 + k)

    def send_back(k):
        arrived(hgrad.at[k, 0, pl.ds(0, chips - 1)], 6 + k)
        hgrad_copy = to_sibling(hgrad.at[k, 0], hgrad.at[k, 1], 16 + k)
        arrived(score.at[k, pl.ds(0, chips - 1)], 8 + k)
        total = score[k, 0]
        for i in range(1, chips):
            total = total + score[k, i]
        mark = jnp.where(
            (iota((8, HALF), 0) == 0) & (iota((8, HALF), 1) == g + high), 1.0, 0.0
        ).astype(BF16)
        score_lane = dot(total.astype(BF16), mark, 0, 0)
        grad_rows = jnp.concatenate([hgrad[k, 0, i] for i in range(chips)], axis=1)
        for s in range(2):
            low = dot(grad_rows, up[s, :HALF, :], 1, 1).astype(BF16)
            hi = (dot(grad_rows, up[s, HALF:, :], 1, 1) + score_lane).astype(BF16)
            stack = jnp.concatenate(
                [low[:, :QUARTER], low[:, QUARTER:], hi[:, :QUARTER], hi[:, QUARTER:]], axis=0
            )
            ret[k, s] = dot(take, stack, 0, 0).astype(BF16).reshape(blocks, MSG, QUARTER)

        def remote_back(s, core, b):
            return pltpu.make_async_remote_copy(
                src_ref=ret.at[k, s, b // 2],
                dst_ref=back.at[k, g],
                send_sem=send_sem.at[20 + k],
                recv_sem=recv_sem.at[20 + k],
                device_id=(core, b),
                device_id_type=MESH,
            )

        def body(i, carry):
            first = far_first(i) * ROW + c
            for b in (first, first + 2):
                remote_back(0, d, b).start()
                remote_back(1, sib, b).start()
            return carry

        lax.fori_loop(0, rings - 1, body, 0)
        first = z * ROW + c
        other = z * ROW + lax.rem(x + 2, ROW)
        beside = z * ROW + lax.rem(x + 1, ROW)
        across = z * ROW + lax.rem(x + 3, ROW)

        @pl.when(c == parity)
        def _():
            remote_back(0, d, other).start()
            remote_back(1, sib, other).start()
            remote_back(1, sib, g).start()
            pltpu.make_async_copy(ret.at[k, 0, g // 2], back.at[k, g], recv_sem.at[20 + k]).start()

        @pl.when(c != parity)
        def _():
            for b in (beside, across):
                remote_back(0, d, b).start()
                remote_back(1, sib, b).start()

        return hgrad_copy

    def combine(k):
        arrived(back.at[k], 20 + k)
        lines_back = back[k].reshape(experts * MSG, QUARTER)
        for q in range(FIELDS):
            term = dot(lines_back, placed[k, :, q * block : (q + 1) * block], 0, 0)
            combined[q] = term if k == 0 else combined[q] + term

    gate_0, x_copy_0, dy_copy_0 = received(0)
    gate_1, x_copy_1, dy_copy_1 = received(1)
    activate(0, gate_0)
    activate(1, gate_1)
    share_act(0)
    share_act(1)
    hgrad_copy_0 = send_back(0)
    hgrad_copy_1 = send_back(1)

    def weight_grad(rows, factor, target):
        left = jnp.concatenate([rows[k, i] for k in range(PARTS) for i in range(2)], axis=0)
        for n in range(ff // STEP):
            units = range(n * (STEP // unit), (n + 1) * (STEP // unit))
            right = jnp.concatenate(
                [
                    jnp.concatenate(
                        [factor[k, i, u] for k in range(PARTS) for i in range(2)], axis=0
                    )
                    for u in units
                ],
                axis=1,
            )
            target[:, pl.ds(n * STEP, STEP)] = dot(left, right, 0, 0)[:feat].astype(BF16)

    for copy in (x_copy_0, x_copy_1, hgrad_copy_0, hgrad_copy_1):
        copy.wait()
    weight_grad(rows_x, hgrad, gup_ref)
    gup_copy = pltpu.make_async_copy(gup_ref, gup_hbm, load_sem.at[6])
    gup_copy.start()
    actg_copies = []
    for k in range(PARTS):
        arrived(actg.at[k, 0, pl.ds(0, chips - 1)], 10 + k)
        actg_copies.append(to_sibling(actg.at[k, 0], actg.at[k, 1], 18 + k))
    combine(0)
    for copy in (dy_copy_0, dy_copy_1, *actg_copies):
        copy.wait()
    weight_grad(rows_dy, actg, gdown_ref)
    gdown_copy = pltpu.make_async_copy(gdown_ref, gdown_hbm, load_sem.at[7])
    gdown_copy.start()

    combine(1)
    for q in range(FIELDS - 1):
        gtok_ref[q * QUARTER : (q + 1) * QUARTER, :] = combined[q].astype(BF16)
    rest = feat - (FIELDS - 1) * QUARTER
    gtok_ref[(FIELDS - 1) * QUARTER :, :] = combined[FIELDS - 1, :rest].astype(BF16)
    summed = combined[FIELDS - 1, rest:]
    found = jnp.zeros((top, block), F32)
    for k in range(top):
        value = jnp.sum(
            jnp.where(ids[k : k + 1, :] == number_hi, summed, 0.0), axis=0, keepdims=True
        )
        found = found + jnp.where(iota((top, block), 0) == k, value, 0.0)
    gprob_ref[...] = found.astype(BF16)

    gup_copy.wait()
    gdown_copy.wait()
    for k in range(PARTS):
        for n, buffer in ((k, send), (20 + k, back)):

            @pl.when(c == parity)
            def _(n=n, buffer=buffer, k=k):
                sent(buffer.at[k, pl.ds(0, experts - 1)], n)

            @pl.when(c != parity)
            def _(n=n, buffer=buffer, k=k):
                sent(buffer.at[k], n)

        for n, buffer in ((4, sums.at[k]), (6, hgrad.at[k, 0]), (8, score.at[k]), (10, actg.at[k, 0])):
            sent(buffer.at[pl.ds(0, chips - 1)], n + k)


def hand_over(*refs):
    count = len(refs) // 3
    source, target, middle = refs[:count], refs[count : 2 * count], refs[2 * count : 3 * count]
    sem = refs[-1]
    loads = [pltpu.make_async_copy(source[n], middle[n], sem.at[0, n]) for n in range(count)]
    stores = [pltpu.make_async_copy(middle[n], target[n], sem.at[1, n]) for n in range(count)]
    for load in loads:
        load.start()
    for load, store in zip(loads, stores):
        load.wait()
        store.start()
    for store in stores:
        store.wait()


def on_device(tokens, cotangent, expert_ids, route_probs, w_up, w_down):
    experts = lax.axis_size("expert")
    chips = lax.axis_size("dp") // 2
    block, feat = tokens.shape
    top = expert_ids.shape[1]
    ff = w_up.shape[2]
    blocks = experts // 2
    count = blocks * SUB
    unit = ff // chips
    wide = 2 * HALF
    vmem = pl.BlockSpec(memory_space=pltpu.VMEM)
    anywhere = pl.BlockSpec(memory_space=pl.ANY)
    results = pl.pallas_call(
        functools.partial(kernel, experts, chips),
        out_shape=(
            jax.ShapeDtypeStruct((feat, block), BF16),
            jax.ShapeDtypeStruct((top, block), BF16),
            jax.ShapeDtypeStruct((feat, ff), BF16),
            jax.ShapeDtypeStruct((feat, ff), BF16),
        ),
        in_specs=[anywhere] * 6,
        out_specs=[vmem] * 2 + [anywhere] * 2,
        scratch_shapes=[
            pltpu.VMEM((feat, block), BF16),
            pltpu.VMEM((feat, block), BF16),
            pltpu.VMEM((top, block), jnp.int32),
            pltpu.VMEM((top, block), BF16),
            pltpu.VMEM((PARTS, experts, MSG, HALF), BF16),
            pltpu.VMEM((PARTS, 2, blocks, MSG, HALF), BF16),
            pltpu.VMEM((2, wide, ff), BF16),
            pltpu.VMEM((2, wide, ff), BF16),
            pltpu.VMEM((PARTS, 3, count, wide), BF16),
            pltpu.VMEM((PARTS, 3, count, wide), BF16),
            pltpu.VMEM((PARTS, chips, 2 * count, unit), BF16),
            pltpu.VMEM((PARTS, chips, 2 * count, unit), F32),
            pltpu.VMEM((PARTS, chips, 2 * count, unit), BF16),
            pltpu.VMEM((PARTS, 2, chips, count, unit), BF16),
            pltpu.VMEM((PARTS, 2, chips, count, unit), BF16),
            pltpu.VMEM((PARTS, chips, 8, count), F32),
            pltpu.VMEM((PARTS, 2, blocks, MSG, QUARTER), BF16),
            pltpu.VMEM((PARTS, experts, MSG, QUARTER), BF16),
            pltpu.VMEM((PARTS, experts * MSG, FIELDS * block), BF16),
            pltpu.VMEM((FIELDS, QUARTER, block), F32),
            pltpu.VMEM((feat, ff), BF16),
            pltpu.VMEM((feat, ff), BF16),
            pltpu.SemaphoreType.DMA((8,)),
            pltpu.SemaphoreType.DMA((22,)),
            pltpu.SemaphoreType.DMA((22,)),
        ],
        compiler_params=pltpu.CompilerParams(
            collective_id=0, has_side_effects=True, vmem_limit_bytes=56 * 2**20
        ),
        name="expert_backward",
    )(tokens.T, cotangent.T, expert_ids.T, route_probs.T, w_up[0], w_down[0].T)
    grad_tokens, grad_probs, grad_up, grad_down = pl.pallas_call(
        hand_over,
        out_shape=tuple(jax.ShapeDtypeStruct(r.shape, r.dtype) for r in results),
        in_specs=[anywhere] * 4,
        out_specs=[anywhere] * 4,
        scratch_shapes=[pltpu.VMEM(r.shape, r.dtype) for r in results] + [pltpu.SemaphoreType.DMA((2, 4))],
        name="hand_over",
    )(*results)
    return (grad_tokens.T, grad_probs.T, grad_up[None], grad_down.T[None])


def solution(mesh):
    in_specs = (
        P("expert", "dp"),
        P("expert", "dp"),
        P("expert", None),
        P("expert", None),
        P("expert", "dp", None),
        P("expert", None, "dp"),
    )
    out_specs = (
        P("expert", "dp"),
        P("expert", None),
        P("expert", "dp", None),
        P("expert", None, "dp"),
    )
    return jax.shard_map(
        on_device, mesh=mesh, in_specs=in_specs, out_specs=out_specs, check_vma=False
    )
```
